32 devices in a mesh: tiles: 8 (over z, y), rep: 4 (over x, core).
Axes of the slice: x: 2, y: 2, z: 4, core: 2. Of those that a mesh axis runs over, the one named last changes fastest.
Arguments:
- trailing_tiles: float32 [4800, 256, 256], P(('tiles', 'rep')), may hold values from -6 to 6
- panel_rows: float32 [96, 256, 512], P('tiles'), may hold values from -3 to 3
- pivot_blocks: float32 [2, 256, 256], replicated
- coupling: float32 [256, 256], replicated, may hold values from -0.1875 to 0.1875
- row_ids: int32 [96], replicated, may hold values from 2 to 96, as said below
- membership: int32 [8, 106], replicated, may hold values from 2 to 96, as said below
- tile_pairs: int32 [4800, 2], P(('tiles', 'rep')), may hold values from 0 to 106, as said below
Outputs:
- updated_tiles: float32 [4800, 256, 256], P(('tiles', 'rep'))
- factors: float32 [96, 256, 512], P('tiles')
- pivot_diag: float32 [2, 256], replicated
The draws below stay inside these ranges and needn't reach their ends.
Inputs may be any that keep to these rules, and one draw needn't show every extreme that they name: `row_ids`: each row block 2 to 95 stands in exactly one slot; the other slots hold 96. `membership`: entries are row blocks 2 to 95, or 96 for none. `tile_pairs`: a slot's first entry is below 12, its second from 12 to 105, or both are 106 for an empty slot; over all devices every unordered pair of row blocks 2 to 96 - 1 (a block with itself too) is listed exactly once; some device fills all 150 slots.
All inputs are finite; a program needn't handle non-finite values.
Results may differ from the reference program's by a relative error of at most 0.00005.
Values sent between devices are 32-bit elements; how exact they have to be, the bound alone decides.
A program may use at most 384 MiB of HBM per device.

```python
import math
import jax
import jax.numpy as jnp
from jax import lax

B = 256
NB = 96
GRIDP = 8
NT = 94
GQ = 1
KB = 12
KQ = 94
NEEDG = 106
RPD = 12
SLOTS = 150
N_TILES = 8
N_REP = 4


def layout_tables(key):
    layout_key = jax.random.fold_in(key, 7)
    perm_key, order_key, turn_key = jax.random.split(layout_key, 3)
    labels = jax.random.permutation(perm_key, NT) + 2
    padded = jnp.concatenate([labels, jnp.full((1,), NB)]).astype(jnp.int32)
    groups = jnp.arange(N_TILES)
    row_class = groups // GQ
    col_class = groups % GQ
    upper_label = jnp.arange(KB)[None, :] * GRIDP + row_class[:, None]
    lower_label = jnp.arange(KQ)[None, :] * GQ + col_class[:, None]
    row_part = padded[jnp.minimum(upper_label, NT)]
    col_part = padded[jnp.minimum(lower_label, NT)]
    membership = jnp.concatenate([row_part, col_part], axis=1).astype(jnp.int32)
    usable = (upper_label[:, :, None] < NT) & (lower_label[:, None, :] <= upper_label[:, :, None])
    usable = usable.reshape(N_TILES, KB * KQ)
    scores = jax.random.randint(order_key, (N_TILES, KB * KQ), 0, 65536) * (KB * KQ) + jnp.arange(KB * KQ)[None, :]
    ordering = jnp.argsort(scores, axis=1)
    picked = jnp.take_along_axis(usable, ordering, axis=1)
    ranking = jnp.cumsum(picked.astype(jnp.int32), axis=1) - 1
    offset = jax.random.randint(turn_key, (N_TILES, 1), 0, N_REP)
    replica = (ranking + offset) % N_REP
    spare_slot = N_TILES * N_REP * SLOTS
    target = (groups[:, None] * N_REP + replica) * SLOTS + ranking // N_REP
    target = jnp.where(picked, target, spare_slot)
    entries = jnp.stack([ordering // KQ, KB + ordering % KQ], axis=-1).astype(jnp.int32)
    pair_table = jnp.full((spare_slot + 1, 2), NEEDG, jnp.int32).at[target.reshape(-1)].set(entries.reshape(-1, 2))
    return (membership, pair_table[:spare_slot])


def draw_membership(key, part):
    return layout_tables(key)[0]


def draw_tile_pairs(key, part):
    return layout_tables(key)[1]


def draw_row_ids(key, part):
    shuffle = jax.random.permutation(jax.random.fold_in(key, 11), N_TILES * RPD)
    return jnp.where(shuffle < NT, shuffle + 2, NB).astype(jnp.int32)


def draw_pivot_blocks(key, part):
    noise_key, diag_key = jax.random.split(jax.random.fold_in(key, 3))
    noise_part = jax.random.normal(noise_key, (2, B, B), jnp.float32)
    levels = jnp.exp(jax.random.uniform(diag_key, (2, B), jnp.float32, math.log(3.0), math.log(6.0)))
    spread = (noise_part + jnp.swapaxes(noise_part, 1, 2)) * (0.85 / math.sqrt(B))
    return spread + levels[:, :, None] * jnp.eye(B, dtype=jnp.float32)[None]


def block_scale(rng, extent, cuts, least, largest):
    gain, own = 1.0, jax.random.fold_in(rng, 6)
    for axis_at, blocks in cuts:
        draws = jnp.exp(jax.random.uniform(jax.random.fold_in(own, axis_at), (blocks,), jnp.float32, least / len(cuts), largest / len(cuts)))
        gain = gain * jnp.repeat(draws, extent[axis_at] // blocks).reshape([-1 if axis == axis_at else 1 for axis in range(len(extent))])
    return gain


def noise(key, dims, scale, reach, shards=(), held_as=jnp.bfloat16):
    drawn = jax.random.normal(key, dims, jnp.float32) * scale
    if len(shards) > 0:
        drawn = block_scale(key, dims, shards, -0.22, 0.18) * drawn
    return jnp.clip(drawn, min=-reach, max=reach).astype(held_as)


def setup_inputs(seed: int = 0) -> dict:
    arg_keys = jax.random.split(jax.random.key(seed), 8)
    trailing_tiles = noise(arg_keys[0], (N_TILES * N_REP * SLOTS, B, B), 1.0, 6.0, ((0, 32),), jnp.float32)
    panel_rows = noise(arg_keys[1], (N_TILES * RPD, B, 2 * B), 0.5, 3.0, ((0, 8),), jnp.float32)
    pivot_blocks = draw_pivot_blocks(jax.random.fold_in(arg_keys[7], 71), 0)
    coupling = noise(arg_keys[3], (B, B), (4 * B) ** -0.5, 0.1875, (), jnp.float32)
    row_ids = draw_row_ids(jax.random.fold_in(arg_keys[7], 71), 0)
    membership = draw_membership(jax.random.fold_in(arg_keys[7], 71), 0)
    tile_pairs = draw_tile_pairs(jax.random.fold_in(arg_keys[7], 71), 0)
    return dict(trailing_tiles=trailing_tiles, panel_rows=panel_rows, pivot_blocks=pivot_blocks, coupling=coupling, row_ids=row_ids, membership=membership, tile_pairs=tile_pairs)


def pivot_factor(matrix):
    lower_factor = jnp.linalg.cholesky(matrix)
    pivots = jnp.diagonal(lower_factor)
    identity = jnp.eye(matrix.shape[0], dtype=matrix.dtype)
    inverse = jax.scipy.linalg.solve_triangular(lower_factor, identity, lower=True)
    return (inverse.T / pivots[None, :], pivots * pivots)

def panel_factors(panel_rows, pivot_blocks, coupling, usable):
    panel_width = pivot_blocks.shape[1]
    solve_one, diag_one = pivot_factor(pivot_blocks[0])
    coupled = jnp.dot(coupling, solve_one, precision=lax.Precision.HIGHEST)
    schur = pivot_blocks[1] - jnp.dot(coupled * diag_one[None, :], coupled.T, precision=lax.Precision.HIGHEST)
    solve_two, diag_two = pivot_factor(schur)
    first = jnp.einsum('rik,kj->rij', panel_rows[:, :, :panel_width], solve_one, precision=lax.Precision.HIGHEST)
    second_raw = panel_rows[:, :, panel_width:] - jnp.einsum('rik,jk->rij', first * diag_one[None, None, :], coupled, precision=lax.Precision.HIGHEST)
    second = jnp.einsum('rik,kj->rij', second_raw, solve_two, precision=lax.Precision.HIGHEST)
    joined = jnp.concatenate([first, second], axis=2)
    factors = jnp.where(usable[:, None, None], joined, jnp.zeros_like(joined))
    return (factors, diag_one, diag_two)

def reference(trailing_tiles, panel_rows, pivot_blocks, coupling, row_ids, membership, tile_pairs):
    factors, diag_one, diag_two = panel_factors(panel_rows, pivot_blocks, coupling, row_ids < NB)
    scales = jnp.concatenate([diag_one, diag_two])
    panel_width = pivot_blocks.shape[1]
    placed = jnp.zeros((NB + 1, panel_width, 2 * panel_width), factors.dtype).at[row_ids].set(factors)
    extended = jnp.concatenate([membership, jnp.full((N_TILES, 1), NB, membership.dtype)], axis=1)
    tiles_grouped = trailing_tiles.reshape(N_TILES, N_REP * SLOTS, panel_width, panel_width)
    pairs_grouped = tile_pairs.reshape(N_TILES, N_REP * SLOTS, 2)

    def one_group(operands):
        tile_block, pair_block, listed = operands
        left_rows = placed[listed[pair_block[:, 0]]] * scales[None, None, :]
        right_rows = placed[listed[pair_block[:, 1]]]
        return tile_block - jnp.einsum('sik,sjk->sij', left_rows, right_rows, precision=lax.Precision.HIGHEST)
    updated = lax.map(one_group, (tiles_grouped, pairs_grouped, extended))
    return (updated.reshape(trailing_tiles.shape), factors, jnp.stack([diag_one, diag_two]))
```

```python
import functools

import jax
import jax.numpy as jnp
from jax import lax
from jax.experimental import pallas as pl
from jax.experimental.pallas import tpu as pltpu
from jax.sharding import PartitionSpec as P

NB = 96
LEFT = 12
HI = lax.Precision.HIGHEST
MESH = pl.DeviceIdType.MESH
MINE, SHARED, OTHER = 0, 1, 2


def pivot_factor(matrix):
    lower_factor = jnp.linalg.cholesky(matrix)
    pivots = jnp.diagonal(lower_factor)
    identity = jnp.eye(matrix.shape[0], dtype=matrix.dtype)
    inverse = jax.scipy.linalg.solve_triangular(lower_factor, identity, lower=True)
    return (inverse.T / pivots[None, :], pivots * pivots)


def pivot_transform(pivot_blocks, coupling):
    dot = functools.partial(jnp.dot, precision=HI)
    solve_one, diag_one = pivot_factor(pivot_blocks[0])
    coupled = dot(coupling, solve_one)
    scaled = coupled * diag_one[None, :]
    schur = pivot_blocks[1] - dot(scaled, coupled.T)
    solve_two, diag_two = pivot_factor(schur)
    corner = -dot(dot(solve_one, scaled.T), solve_two)
    top = jnp.concatenate([solve_one, corner], axis=1)
    bottom = jnp.concatenate([jnp.zeros_like(solve_two), solve_two], axis=1)
    return jnp.concatenate([top, bottom], axis=0), jnp.stack([diag_one, diag_two])


def spread_kernel(sizes, panel, out, z_send, z_recv, y_send, y_recv, x_send, x_recv, c_send, c_recv, own_sem):
    nz, rows, half, alone, shared = sizes
    tile, rep = lax.axis_index("tiles"), lax.axis_index("rep")
    z, y = tile // 2, tile % 2
    x, core = rep // 2, rep % 2
    items = [(0, 0)] + [(s, way) for s in range(1, nz) for way in (0, 1)]
    number = {item: at for at, item in enumerate(items)}

    def there(item):
        step, way = item
        if step == 0:
            return None
        return z - step >= 0 if way == 0 else z + step < nz

    def place(item):
        step, way = item
        return z - step if way == 0 else z + step

    def when(cond, body):
        if cond is None:
            body()
        else:
            pl.when(cond)(body)

    def both(a, b):
        return b if a is None else jnp.logical_and(a, b)

    def offset(part):
        if part == MINE:
            return core * half + x * (alone + shared), alone
        if part == SHARED:
            return core * half + alone, shared
        return core * half + (1 - x) * (alone + shared), alone

    def piece(column, item, part):
        start, size = offset(part)
        if column == 0 and item == (0, 0):
            return panel.at[pl.ds(pl.multiple_of(start, 8), size)]
        return landing(column, item, part)

    def landing(column, item, part):
        start, size = offset(part)
        owner = place(item) * 2 + (y if column == 0 else 1 - y)
        return out.at[pl.ds(pl.multiple_of(owner * rows + start, 8), size)]

    def copy(column, item, part, send, recv, target):
        return pltpu.make_async_remote_copy(
            src_ref=piece(column, item, part), dst_ref=landing(column, item, part),
            send_sem=send, recv_sem=recv, device_id=target, device_id_type=MESH,
        )

    def z_copy(step, way, part):
        at = ((step - 1) * 2 + way) * 2 + part
        item = (step - 1, way if step > 1 else 0)
        target = (tile + 2 if way == 0 else tile - 2, rep)
        return copy(0, item, part, z_send.at[at], z_recv.at[at], target)

    def z_sends(step, way):
        room = z + 1 < nz if way == 0 else z >= 1
        return both(there((step - 1, way)), room)

    def z_arrival(step, way, part):
        at = ((step - 1) * 2 + way) * 2 + part
        return copy(0, (step, way), part, z_send.at[at], z_recv.at[at], (tile, rep))

    def y_copy(column, item, part):
        at = number[item] * 2 + part
        return copy(column, item, part, y_send.at[at], y_recv.at[at], (z * 2 + 1 - y, rep))

    def x_copy(column, item, part=MINE):
        at = column * len(items) + number[item]
        return copy(column, item, part, x_send.at[at], x_recv.at[at], (tile, (1 - x) * 2 + core))

    def c_copy(column, item, part):
        at = (column * len(items) + number[item]) * 3 + part
        return copy(column, item, part, c_send.at[at], c_recv.at[at], (tile, x * 2 + 1 - core))

    def c_arrival(column, item, part):
        at = (column * len(items) + number[item]) * 3 + part
        start, size = offset(part)
        start = start + (1 - 2 * core) * half
        owner = place(item) * 2 + (y if column == 0 else 1 - y)
        ref = out.at[pl.ds(pl.multiple_of(owner * rows + start, 8), size)]
        return pltpu.make_async_remote_copy(
            src_ref=ref, dst_ref=ref, send_sem=c_send.at[at], recv_sem=c_recv.at[at],
            device_id=(tile, x * 2 + 1 - core), device_id_type=MESH,
        )

    barrier = pltpu.get_barrier_semaphore()

    def greet(target):
        pl.semaphore_signal(barrier, inc=1, device_id=target, device_id_type=MESH)

    greet((z * 2 + 1 - y, rep))
    greet((tile, (1 - x) * 2 + core))
    greet((tile, x * 2 + 1 - core))
    pl.when(z >= 1)(lambda: greet((tile - 2, rep)))
    pl.when(z + 1 < nz)(lambda: greet((tile + 2, rep)))
    peers = 3 + jnp.where(z >= 1, 1, 0) + jnp.where(z + 1 < nz, 1, 0)
    pl.semaphore_wait(barrier, peers)

    for part in (MINE, SHARED):
        for way in (0, 1):
            if nz > 1:
                when(z_sends(1, way), lambda: z_copy(1, way, part).start())
        y_copy(0, (0, 0), part).start()
    own = pltpu.make_async_copy(panel, out.at[pl.ds(pl.multiple_of(tile * rows, 8), rows)], own_sem)
    own.start()

    def on_z(step, way, part):
        item = (step, way)

        def body():
            z_arrival(step, way, part).wait_recv()
            if step + 1 < nz:
                when(z_sends(step + 1, way), lambda: z_copy(step + 1, way, part).start())
            y_copy(0, item, part).start()
            if part == MINE:
                x_copy(0, item).start()
            c_copy(0, item, part).start()

        when(there(item), body)

    def on_y(item, part):
        def body():
            y_copy(1, item, part).wait_recv()
            if part == MINE:
                x_copy(1, item).start()
            c_copy(1, item, part).start()

        when(there(item), body)

    def on_x(column, item):
        def body():
            x_copy(column, item, OTHER).wait_recv()
            c_copy(column, item, OTHER).start()

        when(there(item), body)

    def at_step(step):
        return [item for item in items if item[0] == step]

    for step in range(1, nz + 1):
        for part in (MINE, SHARED):
            if step < nz:
                for way in (0, 1):
                    on_z(step, way, part)
            for item in at_step(step - 1):
                on_y(item, part)
        if step < nz:
            for item in at_step(step - 1):
                if step > 1:
                    on_x(0, item)
            for item in at_step(step - 2):
                on_x(1, item)
    for item in at_step(nz - 1):
        on_x(0, item)
    for step in (nz - 2, nz - 1):
        for item in at_step(step):
            on_x(1, item)

    for column in (0, 1):
        for item in items:
            if column == 0 and item == (0, 0):
                continue

            def finish():
                for part in (MINE, SHARED, OTHER):
                    c_arrival(column, item, part).wait_recv()
                    c_copy(column, item, part).wait_send()
                x_copy(column, item).wait_send()

            when(there(item), finish)
    for item in items:
        for part in (MINE, SHARED):
            when(there(item), lambda: y_copy(0, item, part).wait_send())
            for way in (0, 1):
                if item[0] + 1 < nz and (item[0] == 0 or item[1] == way):
                    step = item[0] + 1
                    when(z_sends(step, way), lambda: z_copy(step, way, part).wait_send())
    own.wait()


def spread(panel, mesh):
    n_tiles, n_rep = mesh.shape["tiles"], mesh.shape["rep"]
    assert n_tiles % 2 == 0 and n_rep == 4
    nz = n_tiles // 2
    rows, width = panel.shape
    half = rows // 2
    alone = half // 24 * 8
    sizes = (nz, rows, half, alone, half - 2 * alone)
    n_items = 2 * nz - 1
    dma = lambda n: pltpu.SemaphoreType.DMA((n,))
    return pl.pallas_call(
        functools.partial(spread_kernel, sizes),
        out_shape=jax.ShapeDtypeStruct((n_tiles * rows, width), panel.dtype),
        in_specs=[pl.BlockSpec(memory_space=pl.ANY)],
        out_specs=pl.BlockSpec(memory_space=pl.ANY),
        scratch_shapes=[dma(4 * max(nz - 1, 1))] * 2 + [dma(2 * n_items)] * 2 + [dma(2 * n_items)] * 2
        + [dma(6 * n_items)] * 2 + [pltpu.SemaphoreType.DMA],
        compiler_params=pltpu.CompilerParams(collective_id=0, has_side_effects=True),
        name="spread_rows",
    )(panel)


def halves(value):
    high = value.astype(jnp.bfloat16)
    low = (value - high.astype(jnp.float32)).astype(jnp.bfloat16)
    return high, low


def left_kernel(source, rows, gram, out):
    product = lax.dot_general(rows[0], gram[...], (((1,), (0,)), ((), ())), precision=HI,
                              preferred_element_type=jnp.float32)
    high, low = halves(product)
    out[0] = jnp.concatenate([high, high, low], axis=1)


def left_rows(every_row, gram, source):
    block, width = every_row.shape[1:]
    return pl.pallas_call(
        left_kernel,
        grid_spec=pltpu.PrefetchScalarGridSpec(
            num_scalar_prefetch=1, grid=(source.shape[0],),
            in_specs=[
                pl.BlockSpec((1, block, width), lambda i, src: (src[i], 0, 0)),
                pl.BlockSpec((width, width), lambda i, src: (0, 0)),
            ],
            out_specs=pl.BlockSpec((1, block, 3 * width), lambda i, src: (i, 0, 0)),
        ),
        out_shape=jax.ShapeDtypeStruct((source.shape[0], block, 3 * width), jnp.bfloat16),
        compiler_params=pltpu.CompilerParams(vmem_limit_bytes=32 << 20),
        name="left_rows",
    )(source, every_row, gram)


def update_kernel(per_step, left, right, used, tiles, weights, *refs):
    rows, out = refs[:per_step], refs[per_step]
    step = pl.program_id(0)
    for at in range(per_step):
        slot = step * per_step + at
        high, low = halves(rows[at][0])
        other = jnp.concatenate([high, low, high], axis=1)
        product = lax.dot_general(weights[left[slot]], other, (((1,), (1,)), ((), ())),
                                  preferred_element_type=jnp.float32)
        out[at] = tiles[at] - jnp.where(used[slot] > 0, product, jnp.zeros_like(product))


def update(tiles, weights, every_row, left, right, used):
    slots, block, _ = tiles.shape
    width = every_row.shape[2]
    per_step = next(n for n in (5, 4, 3, 2, 1) if slots % n == 0)
    row_spec = lambda at: pl.BlockSpec((1, block, width), lambda i, l, r, u: (r[i * per_step + at], 0, 0))
    tile_spec = pl.BlockSpec((per_step, block, block), lambda i, l, r, u: (i, 0, 0))
    return pl.pallas_call(
        functools.partial(update_kernel, per_step),
        grid_spec=pltpu.PrefetchScalarGridSpec(
            num_scalar_prefetch=3, grid=(slots // per_step,),
            in_specs=[tile_spec, pl.BlockSpec(weights.shape, lambda i, l, r, u: (0, 0, 0))]
            + [row_spec(at) for at in range(per_step)],
            out_specs=tile_spec,
        ),
        out_shape=jax.ShapeDtypeStruct(tiles.shape, tiles.dtype),
        compiler_params=pltpu.CompilerParams(vmem_limit_bytes=56 << 20),
        name="update_tiles",
    )(left, right, used, tiles, weights, *[every_row] * per_step)


def per_device(mesh, trailing_tiles, panel_rows, pivot_blocks, coupling, row_ids, membership, tile_pairs):
    owned, block, width = panel_rows.shape
    tile_index = lax.axis_index("tiles")
    own_ids = lax.dynamic_slice_in_dim(row_ids, tile_index * owned, owned)
    wanted = lax.dynamic_index_in_dim(membership, tile_index, 0, keepdims=False)
    source = jnp.argmax(row_ids[None, :] == wanted[:, None], axis=1).astype(jnp.int32)
    listed = jnp.concatenate([wanted < NB, jnp.zeros((1,), bool)])
    source = jnp.concatenate([source, jnp.zeros((1,), jnp.int32)])
    left, right = tile_pairs[:, 0], tile_pairs[:, 1]
    used = (listed[left] & listed[right]).astype(jnp.int32)
    every_row = spread(panel_rows.reshape(owned * block, width), mesh).reshape(-1, block, width)
    transform, diagonal = pivot_transform(pivot_blocks, coupling)
    factors = jnp.einsum("rik,kj->rij", panel_rows, transform, precision=HI)
    factors = jnp.where((own_ids < NB)[:, None, None], factors, jnp.zeros_like(factors))
    gram = jnp.dot(transform * diagonal.reshape(1, -1), transform.T, precision=HI)
    weights = left_rows(every_row, gram, source[:LEFT])
    updated = update(trailing_tiles, weights, every_row, jnp.minimum(left, LEFT - 1), source[right], used)
    return (updated, factors, diagonal)


def solution(mesh):
    return jax.shard_map(
        functools.partial(per_device, mesh),
        mesh=mesh,
        in_specs=(
            P(("tiles", "rep"), None, None),
            P("tiles", None, None),
            P(),
            P(),
            P(),
            P(),
            P(("tiles", "rep"), None),
        ),
        out_specs=(P(("tiles", "rep"), None, None), P("tiles", None, None), P()),
        check_vma=False,
    )
```

```python
import functools

import jax
import jax.numpy as jnp
from jax import lax
from jax.experimental import pallas as pl
from jax.experimental.pallas import tpu as pltpu
from jax.sharding import PartitionSpec as P

NB = 96
LEFT = 12
HI = lax.Precision.HIGHEST
MESH = pl.DeviceIdType.MESH
MINE, SHARED, OTHER = 0, 1, 2


def matmul(left, right, turned=False):
    return lax.dot_general(left, right, (((1,), (1 if turned else 0,)), ((), ())), precision=HI,
                           preferred_element_type=jnp.float32)


def pivot_stages(pivot_blocks, coupling, inverse, diagonal, work, lower, schur, solve, coupled):
    block = coupling.shape[0]
    h = block // 2
    quarter = h // 4

    def identity():
        return lax.broadcasted_iota(jnp.int32, (h, h), 0) == lax.broadcasted_iota(jnp.int32, (h, h), 1)

    def begin(matrix):
        work[:, :h] = matrix
        work[:, h:] = identity().astype(jnp.float32)

    def eliminate(part):
        first = part * quarter
        lane = lax.broadcasted_iota(jnp.int32, (h - first, h), 1)
        below = lax.broadcasted_iota(jnp.int32, (h - first, 1), 0) + first
        lane_row = lax.broadcasted_iota(jnp.int32, (1, h), 1)

        def step(j, carry):
            row = work[pl.ds(j, 1), :]
            rest = work[first:, :]
            column = jnp.sum(jnp.where(lane == j, rest[:, :h], 0.0), axis=1, keepdims=True)
            pivot = jnp.sum(jnp.where(lane_row == j, row[:, :h], 0.0), axis=1, keepdims=True)
            work[first:, :] = rest - jnp.where(below > j, column / pivot, 0.0) * row
            return carry

        lax.fori_loop(first, first + quarter, step, 0)

    def result():
        picked = jnp.where(identity(), work[:, :h], 0.0)
        return (work[:, h:], jnp.sum(picked, axis=0, keepdims=True), jnp.sum(picked, axis=1, keepdims=True))

    def pivot(at, source):
        base = at * block

        def middle():
            unit, d_row, d_column = result()
            zero = jnp.zeros((h, h), jnp.float32)
            solve[:h, :h] = unit
            solve[:h, h:] = zero
            inverse[base:base + h, base:base + h] = unit / d_column
            inverse[base:base + h, base + h:base + block] = zero
            diagonal[at:at + 1, :h] = d_row
            scaled = matmul(source()[h:, :h], unit, True)
            lower[...] = scaled / d_row
            begin(source()[h:, h:] - matmul(scaled, lower[...], True))

        def last():
            unit, d_row, d_column = result()
            corner = -matmul(matmul(unit, lower[...]), solve[:h, :h])
            solve[h:, :h] = corner
            solve[h:, h:] = unit
            inverse[base + h:base + block, base:base + h] = corner / d_column
            inverse[base + h:base + block, base + h:base + block] = unit / d_column
            diagonal[at:at + 1, h:] = d_row

        walk = [(5.5, functools.partial(eliminate, part)) for part in range(4)]
        return [(0.5, lambda: begin(source()[:h, :h]))] + walk + [(2, middle)] + walk + [(2, last)]

    def couple():
        coupled[...] = matmul(coupling[...], solve[...], True)
        schur[...] = pivot_blocks[1] - matmul(coupled[...], coupled[...] / diagonal[0:1, :], True)

    def join():
        inverse[:block, block:] = jnp.zeros((block, block), jnp.float32)
        mixed = matmul(inverse[block:, block:], coupled[...])
        inverse[block:, :block] = -matmul(mixed, inverse[:block, :block])

    return (pivot(0, lambda: pivot_blocks[0]) + [(3, couple)] + pivot(1, lambda: schur[...]) + [(3, join)])


def spread_kernel(sizes, panel, pivot_blocks, coupling, out, inverse, diagonal, factors,
                  z_send, z_recv, y_send, y_recv, x_send, x_recv, c_send, c_recv, own_sem,
                  work, lower, schur, solve, coupled, rows_in, rows_out, in_sem, out_sem):
    nz, rows, half, alone, shared = sizes
    tile, rep = lax.axis_index("tiles"), lax.axis_index("rep")
    z, y = tile // 2, tile % 2
    x, core = rep // 2, rep % 2
    items = [(0, 0)] + [(s, way) for s in range(1, nz) for way in (0, 1)]
    number = {item: at for at, item in enumerate(items)}

    def there(item):
        step, way = item
        if step == 0:
            return None
        return z - step >= 0 if way == 0 else z + step < nz

    def place(item):
        step, way = item
        return z - step if way == 0 else z + step

    def when(cond, body):
        if cond is None:
            body()
        else:
            pl.when(cond)(body)

    def both(a, b):
        return b if a is None else jnp.logical_and(a, b)

    def offset(part):
        if part == MINE:
            return core * half + x * (alone + shared), alone
        if part == SHARED:
            return core * half + alone, shared
        return core * half + (1 - x) * (alone + shared), alone

    def piece(column, item, part):
        start, size = offset(part)
        if column == 0 and item == (0, 0):
            return panel.at[pl.ds(pl.multiple_of(start, 8), size)]
        return landing(column, item, part)

    def landing(column, item, part):
        start, size = offset(part)
        owner = place(item) * 2 + (y if column == 0 else 1 - y)
        return out.at[pl.ds(pl.multiple_of(owner * rows + start, 8), size)]

    def copy(column, item, part, send, recv, target):
        return pltpu.make_async_remote_copy(
            src_ref=piece(column, item, part), dst_ref=landing(column, item, part),
            send_sem=send, recv_sem=recv, device_id=target, device_id_type=MESH,
        )

    def z_copy(step, way, part):
        at = ((step - 1) * 2 + way) * 2 + part
        item = (step - 1, way if step > 1 else 0)
        target = (tile + 2 if way == 0 else tile - 2, rep)
        return copy(0, item, part, z_send.at[at], z_recv.at[at], target)

    def z_sends(step, way):
        room = z + 1 < nz if way == 0 else z >= 1
        return both(there((step - 1, way)), room)

    def z_arrival(step, way, part):
        at = ((step - 1) * 2 + way) * 2 + part
        return copy(0, (step, way), part, z_send.at[at], z_recv.at[at], (tile, rep))

    def y_copy(column, item, part):
        at = number[item] * 2 + part
        return copy(column, item, part, y_send.at[at], y_recv.at[at], (z * 2 + 1 - y, rep))

    def x_copy(column, item, part=MINE):
        at = column * len(items) + number[item]
        return copy(column, item, part, x_send.at[at], x_recv.at[at], (tile, (1 - x) * 2 + core))

    def c_copy(column, item, part):
        at = (column * len(items) + number[item]) * 3 + part
        return copy(column, item, part, c_send.at[at], c_recv.at[at], (tile, x * 2 + 1 - core))

    def c_arrival(column, item, part):
        at = (column * len(items) + number[item]) * 3 + part
        start, size = offset(part)
        start = start + (1 - 2 * core) * half
        owner = place(item) * 2 + (y if column == 0 else 1 - y)
        ref = out.at[pl.ds(pl.multiple_of(owner * rows + start, 8), size)]
        return pltpu.make_async_remote_copy(
            src_ref=ref, dst_ref=ref, send_sem=c_send.at[at], recv_sem=c_recv.at[at],
            device_id=(tile, x * 2 + 1 - core), device_id_type=MESH,
        )

    barrier = pltpu.get_barrier_semaphore()

    def greet(target):
        pl.semaphore_signal(barrier, inc=1, device_id=target, device_id_type=MESH)

    greet((z * 2 + 1 - y, rep))
    greet((tile, (1 - x) * 2 + core))
    greet((tile, x * 2 + 1 - core))
    pl.when(z >= 1)(lambda: greet((tile - 2, rep)))
    pl.when(z + 1 < nz)(lambda: greet((tile + 2, rep)))
    peers = 3 + jnp.where(z >= 1, 1, 0) + jnp.where(z + 1 < nz, 1, 0)
    pl.semaphore_wait(barrier, peers)

    for part in (MINE, SHARED):
        for way in (0, 1):
            if nz > 1:
                when(z_sends(1, way), lambda: z_copy(1, way, part).start())
        y_copy(0, (0, 0), part).start()
    own = pltpu.make_async_copy(panel, out.at[pl.ds(pl.multiple_of(tile * rows, 8), rows)], own_sem)
    own.start()

    def on_z(step, way, part):
        item = (step, way)

        def body():
            z_arrival(step, way, part).wait_recv()
            if step + 1 < nz:
                when(z_sends(step + 1, way), lambda: z_copy(step + 1, way, part).start())
            y_copy(0, item, part).start()
            if part == MINE:
                x_copy(0, item).start()
            c_copy(0, item, part).start()

        when(there(item), body)

    def on_y(item, part):
        def body():
            y_copy(1, item, part).wait_recv()
            if part == MINE:
                x_copy(1, item).start()
            c_copy(1, item, part).start()

        when(there(item), body)

    def on_x(column, item):
        def body():
            x_copy(column, item, OTHER).wait_recv()
            c_copy(column, item, OTHER).start()

        when(there(item), body)

    def at_step(step):
        return [item for item in items if item[0] == step]

    block = rows_in.shape[0]

    def solve_rows(at):
        here = pl.ds(at * block, block)
        fetch = pltpu.make_async_copy(panel.at[here], rows_in, in_sem)
        fetch.start()
        fetch.wait()
        rows_out[...] = matmul(rows_in[...], inverse[...], True)
        store = pltpu.make_async_copy(rows_out, factors.at[here], out_sem)
        store.start()
        store.wait()

    stages = pivot_stages(pivot_blocks, coupling, inverse, diagonal, work, lower, schur, solve, coupled)
    stages += [(2.2, functools.partial(solve_rows, at)) for at in range(rows // block)]
    total = sum(weight for weight, _ in stages)
    done, gap = 0.0, 0

    def arithmetic():
        nonlocal done, gap
        gap += 1
        while stages and (done < total * gap / (2 * nz) or gap == 2 * nz):
            weight, stage = stages.pop(0)
            stage()
            done += weight

    for step in range(1, nz + 1):
        for part in (MINE, SHARED):
            arithmetic()
            if step < nz:
                for way in (0, 1):
                    on_z(step, way, part)
            for item in at_step(step - 1):
                on_y(item, part)
        if step < nz:
            for item in at_step(step - 1):
                if step > 1:
                    on_x(0, item)
            for item in at_step(step - 2):
                on_x(1, item)
    for item in at_step(nz - 1):
        on_x(0, item)
    for step in (nz - 2, nz - 1):
        for item in at_step(step):
            on_x(1, item)

    for column in (0, 1):
        for item in items:
            if column == 0 and item == (0, 0):
                continue

            def finish():
                for part in (MINE, SHARED, OTHER):
                    c_arrival(column, item, part).wait_recv()
                    c_copy(column, item, part).wait_send()
                x_copy(column, item).wait_send()

            when(there(item), finish)
    for item in items:
        for part in (MINE, SHARED):
            when(there(item), lambda: y_copy(0, item, part).wait_send())
            for way in (0, 1):
                if item[0] + 1 < nz and (item[0] == 0 or item[1] == way):
                    step = item[0] + 1
                    when(z_sends(step, way), lambda: z_copy(step, way, part).wait_send())
    own.wait()


def spread(panel, pivot_blocks, coupling, mesh):
    n_tiles, n_rep = mesh.shape["tiles"], mesh.shape["rep"]
    assert n_tiles % 2 == 0 and n_rep == 4
    nz = n_tiles // 2
    rows, width = panel.shape
    half = rows // 2
    alone = half // 24 * 8
    sizes = (nz, rows, half, alone, half - 2 * alone)
    n_items = 2 * nz - 1
    dma = lambda n: pltpu.SemaphoreType.DMA((n,))
    block = coupling.shape[0]
    any_space, vmem = pl.BlockSpec(memory_space=pl.ANY), pl.BlockSpec(memory_space=pltpu.VMEM)
    f32 = lambda *shape: jax.ShapeDtypeStruct(shape, jnp.float32)
    buffer = lambda *shape: pltpu.VMEM(shape, jnp.float32)
    return pl.pallas_call(
        functools.partial(spread_kernel, sizes),
        out_shape=(f32(n_tiles * rows, width), f32(width, width), f32(*pivot_blocks.shape[:2]), f32(rows, width)),
        in_specs=[any_space, vmem, vmem],
        out_specs=(any_space, vmem, vmem, any_space),
        scratch_shapes=[dma(4 * max(nz - 1, 1))] * 2 + [dma(2 * n_items)] * 2 + [dma(2 * n_items)] * 2
        + [dma(6 * n_items)] * 2 + [pltpu.SemaphoreType.DMA]
        + [buffer(block // 2, block), buffer(block // 2, block // 2)] + [buffer(block, block)] * 3
        + [buffer(block, width)] * 2 + [pltpu.SemaphoreType.DMA] * 2,
        compiler_params=pltpu.CompilerParams(
            collective_id=0, has_side_effects=True, vmem_limit_bytes=40 << 20),
        name="spread_rows",
    )(panel, pivot_blocks, coupling)


def halves(value):
    high = value.astype(jnp.bfloat16)
    low = (value - high.astype(jnp.float32)).astype(jnp.bfloat16)
    return high, low


def split_product(stacked, right, dims):
    rows = stacked.shape[0] // 2
    high, low = halves(right)
    dot = functools.partial(lax.dot_general, dimension_numbers=(dims, ((), ())), preferred_element_type=jnp.float32)
    first = dot(stacked, high)
    return first[:rows] + (first[rows:] + dot(stacked[:rows], low))


def left_kernel(source, rows, gram, out):
    stacked = jnp.concatenate(halves(rows[0]), axis=0)
    product = split_product(stacked, gram[...], ((1,), (0,)))
    out[0] = jnp.concatenate(halves(product), axis=0)


def left_rows(every_row, gram, source):
    block, width = every_row.shape[1:]
    return pl.pallas_call(
        left_kernel,
        grid_spec=pltpu.PrefetchScalarGridSpec(
            num_scalar_prefetch=1, grid=(source.shape[0],),
            in_specs=[
                pl.BlockSpec((1, block, width), lambda i, src: (src[i], 0, 0)),
                pl.BlockSpec((width, width), lambda i, src: (0, 0)),
            ],
            out_specs=pl.BlockSpec((1, 2 * block, width), lambda i, src: (i, 0, 0)),
        ),
        out_shape=jax.ShapeDtypeStruct((source.shape[0], 2 * block, width), jnp.bfloat16),
        compiler_params=pltpu.CompilerParams(vmem_limit_bytes=32 << 20),
        name="left_rows",
    )(source, every_row, gram)


def update_kernel(per_step, left, right, used, tiles, weights, *refs):
    rows, out = refs[:per_step], refs[per_step]
    step = pl.program_id(0)
    for at in range(per_step):
        slot = step * per_step + at
        product = split_product(weights[left[slot]], rows[at][0], ((1,), (1,)))
        out[at] = tiles[at] - jnp.where(used[slot] > 0, product, jnp.zeros_like(product))


def update(tiles, weights, every_row, left, right, used):
    slots, block, _ = tiles.shape
    width = every_row.shape[2]
    per_step = next(n for n in (5, 4, 3, 2, 1) if slots % n == 0)
    row_spec = lambda at: pl.BlockSpec((1, block, width), lambda i, l, r, u: (r[i * per_step + at], 0, 0))
    tile_spec = pl.BlockSpec((per_step, block, block), lambda i, l, r, u: (i, 0, 0))
    return pl.pallas_call(
        functools.partial(update_kernel, per_step),
        grid_spec=pltpu.PrefetchScalarGridSpec(
            num_scalar_prefetch=3, grid=(slots // per_step,),
            in_specs=[tile_spec, pl.BlockSpec(weights.shape, lambda i, l, r, u: (0, 0, 0))]
            + [row_spec(at) for at in range(per_step)],
            out_specs=tile_spec,
        ),
        out_shape=jax.ShapeDtypeStruct(tiles.shape, tiles.dtype),
        compiler_params=pltpu.CompilerParams(vmem_limit_bytes=56 << 20),
        name="update_tiles",
    )(left, right, used, tiles, weights, *[every_row] * per_step)


def per_device(mesh, trailing_tiles, panel_rows, pivot_blocks, coupling, row_ids, membership, tile_pairs):
    owned, block, width = panel_rows.shape
    tile_index = lax.axis_index("tiles")
    own_ids = lax.dynamic_slice_in_dim(row_ids, tile_index * owned, owned)
    wanted = lax.dynamic_index_in_dim(membership, tile_index, 0, keepdims=False)
    source = jnp.argmax(row_ids[None, :] == wanted[:, None], axis=1).astype(jnp.int32)
    listed = jnp.concatenate([wanted < NB, jnp.zeros((1,), bool)])
    source = jnp.concatenate([source, jnp.zeros((1,), jnp.int32)])
    left, right = tile_pairs[:, 0], tile_pairs[:, 1]
    used = (listed[left] & listed[right]).astype(jnp.int32)
    every_row, inverse, diagonal, factors = spread(
        panel_rows.reshape(owned * block, width), pivot_blocks, coupling, mesh)
    every_row = every_row.reshape(-1, block, width)
    factors = factors.reshape(panel_rows.shape)
    factors = jnp.where((own_ids < NB)[:, None, None], factors, jnp.zeros_like(factors))
    gram = jnp.dot((inverse * diagonal.reshape(-1, 1)).T, inverse, precision=HI)
    weights = left_rows(every_row, gram, source[:LEFT])
    updated = update(trailing_tiles, weights, every_row, jnp.minimum(left, LEFT - 1), source[right], used)
    return (updated, factors, diagonal)


def solution(mesh):
    return jax.shard_map(
        functools.partial(per_device, mesh),
        mesh=mesh,
        in_specs=(
            P(("tiles", "rep"), None, None),
            P("tiles", None, None),
            P(),
            P(),
            P(),
            P(),
            P(("tiles", "rep"), None),
        ),
        out_specs=(P(("tiles", "rep"), None, None), P("tiles", None, None), P()),
        check_vma=False,
    )
```

```python
import functools

import jax
import jax.numpy as jnp
from jax import lax
from jax.experimental import pallas as pl
from jax.experimental.pallas import tpu as pltpu
from jax.sharding import PartitionSpec as P

NB = 96
LEFT = 12
HI = lax.Precision.HIGHEST
MESH = pl.DeviceIdType.MESH
MINE, SHARED, OTHER = 0, 1, 2


def matmul(left, right, turned=False):
    return lax.dot_general(left, right, (((1,), (1 if turned else 0,)), ((), ())), precision=HI,
                           preferred_element_type=jnp.float32)


def pivot_stages(pivot_blocks, coupling, inverse, diagonal, work, lower, schur, solve, coupled):
    block = coupling.shape[0]
    h = block // 2
    quarter = h // 4

    def identity():
        return lax.broadcasted_iota(jnp.int32, (h, h), 0) == lax.broadcasted_iota(jnp.int32, (h, h), 1)

    def begin(matrix):
        work[:, :h] = matrix
        work[:, h:] = identity().astype(jnp.float32)

    def eliminate(part):
        first = part * quarter
        lane = lax.broadcasted_iota(jnp.int32, (h - first, h), 1)
        below = lax.broadcasted_iota(jnp.int32, (h - first, 1), 0) + first
        lane_row = lax.broadcasted_iota(jnp.int32, (1, h), 1)

        def step(j, carry):
            row = work[pl.ds(j, 1), :]
            rest = work[first:, :]
            column = jnp.sum(jnp.where(lane == j, rest[:, :h], 0.0), axis=1, keepdims=True)
            pivot = jnp.sum(jnp.where(lane_row == j, row[:, :h], 0.0), axis=1, keepdims=True)
            work[first:, :] = rest - jnp.where(below > j, column / pivot, 0.0) * row
            return carry

        lax.fori_loop(first, first + quarter, step, 0)

    def result():
        picked = jnp.where(identity(), work[:, :h], 0.0)
        return (work[:, h:], jnp.sum(picked, axis=0, keepdims=True), jnp.sum(picked, axis=1, keepdims=True))

    def pivot(at, source):
        base = at * block

        def middle():
            unit, d_row, d_column = result()
            zero = jnp.zeros((h, h), jnp.float32)
            solve[:h, :h] = unit
            solve[:h, h:] = zero
            inverse[base:base + h, base:base + h] = unit / d_column
            inverse[base:base + h, base + h:base + block] = zero
            diagonal[at:at + 1, :h] = d_row
            scaled = matmul(source()[h:, :h], unit, True)
            lower[...] = scaled / d_row
            begin(source()[h:, h:] - matmul(scaled, lower[...], True))

        def last():
            unit, d_row, d_column = result()
            corner = -matmul(matmul(unit, lower[...]), solve[:h, :h])
            solve[h:, :h] = corner
            solve[h:, h:] = unit
            inverse[base + h:base + block, base:base + h] = corner / d_column
            inverse[base + h:base + block, base + h:base + block] = unit / d_column
            diagonal[at:at + 1, h:] = d_row

        walk = [(5.5, functools.partial(eliminate, part)) for part in range(4)]
        return [(0.5, lambda: begin(source()[:h, :h]))] + walk + [(2, middle)] + walk + [(2, last)]

    def couple():
        coupled[...] = matmul(coupling[...], solve[...], True)
        schur[...] = pivot_blocks[1] - matmul(coupled[...], coupled[...] / diagonal[0:1, :], True)

    def join():
        inverse[:block, block:] = jnp.zeros((block, block), jnp.float32)
        mixed = matmul(inverse[block:, block:], coupled[...])
        inverse[block:, :block] = -matmul(mixed, inverse[:block, :block])

    return (pivot(0, lambda: pivot_blocks[0]) + [(3, couple)] + pivot(1, lambda: schur[...]) + [(3, join)])


def spread_kernel(sizes, panel, pivot_blocks, coupling, out, inverse, diagonal, factors,
                  z_send, z_recv, y_send, y_recv, x_send, x_recv, c_send, c_recv, own_sem,
                  work, lower, schur, solve, coupled, rows_in, rows_out, in_sem, out_sem):
    nz, rows, half, alone, shared = sizes
    tile, rep = lax.axis_index("tiles"), lax.axis_index("rep")
    z, y = tile // 2, tile % 2
    x, core = rep // 2, rep % 2
    items = [(0, 0)] + [(s, way) for s in range(1, nz) for way in (0, 1)]
    number = {item: at for at, item in enumerate(items)}

    def there(item):
        step, way = item
        if step == 0:
            return None
        return z - step >= 0 if way == 0 else z + step < nz

    def place(item):
        step, way = item
        return z - step if way == 0 else z + step

    def when(cond, body):
        if cond is None:
            body()
        else:
            pl.when(cond)(body)

    def both(a, b):
        return b if a is None else jnp.logical_and(a, b)

    def offset(part):
        if part == MINE:
            return core * half + x * (alone + shared), alone
        if part == SHARED:
            return core * half + alone, shared
        return core * half + (1 - x) * (alone + shared), alone

    def piece(column, item, part):
        start, size = offset(part)
        if column == 0 and item == (0, 0):
            return panel.at[pl.ds(pl.multiple_of(start, 8), size)]
        return landing(column, item, part)

    def landing(column, item, part):
        start, size = offset(part)
        owner = place(item) * 2 + (y if column == 0 else 1 - y)
        return out.at[pl.ds(pl.multiple_of(owner * rows + start, 8), size)]

    def copy(column, item, part, send, recv, target):
        return pltpu.make_async_remote_copy(
            src_ref=piece(column, item, part), dst_ref=landing(column, item, part),
            send_sem=send, recv_sem=recv, device_id=target, device_id_type=MESH,
        )

    def z_copy(step, way, part):
        at = ((step - 1) * 2 + way) * 2 + part
        item = (step - 1, way if step > 1 else 0)
        target = (tile + 2 if way == 0 else tile - 2, rep)
        return copy(0, item, part, z_send.at[at], z_recv.at[at], target)

    def z_sends(step, way):
        room = z + 1 < nz if way == 0 else z >= 1
        return both(there((step - 1, way)), room)

    def z_arrival(step, way, part):
        at = ((step - 1) * 2 + way) * 2 + part
        return copy(0, (step, way), part, z_send.at[at], z_recv.at[at], (tile, rep))

    def y_copy(column, item, part):
        at = number[item] * 2 + part
        return copy(column, item, part, y_send.at[at], y_recv.at[at], (z * 2 + 1 - y, rep))

    def x_copy(column, item, part=MINE):
        at = column * len(items) + number[item]
        return copy(column, item, part, x_send.at[at], x_recv.at[at], (tile, (1 - x) * 2 + core))

    def c_copy(column, item, part):
        at = (column * len(items) + number[item]) * 3 + part
        return copy(column, item, part, c_send.at[at], c_recv.at[at], (tile, x * 2 + 1 - core))

    def c_arrival(column, item, part):
        at = (column * len(items) + number[item]) * 3 + part
        start, size = offset(part)
        start = start + (1 - 2 * core) * half
        owner = place(item) * 2 + (y if column == 0 else 1 - y)
        ref = out.at[pl.ds(pl.multiple_of(owner * rows + start, 8), size)]
        return pltpu.make_async_remote_copy(
            src_ref=ref, dst_ref=ref, send_sem=c_send.at[at], recv_sem=c_recv.at[at],
            device_id=(tile, x * 2 + 1 - core), device_id_type=MESH,
        )

    barrier = pltpu.get_barrier_semaphore()

    def greet(target):
        pl.semaphore_signal(barrier, inc=1, device_id=target, device_id_type=MESH)

    greet((z * 2 + 1 - y, rep))
    greet((tile, (1 - x) * 2 + core))
    greet((tile, x * 2 + 1 - core))
    pl.when(z >= 1)(lambda: greet((tile - 2, rep)))
    pl.when(z + 1 < nz)(lambda: greet((tile + 2, rep)))
    peers = 3 + jnp.where(z >= 1, 1, 0) + jnp.where(z + 1 < nz, 1, 0)
    pl.semaphore_wait(barrier, peers)

    for part in (MINE, SHARED):
        for way in (0, 1):
            if nz > 1:
                when(z_sends(1, way), lambda: z_copy(1, way, part).start())
        y_copy(0, (0, 0), part).start()
    own = pltpu.make_async_copy(panel, out.at[pl.ds(pl.multiple_of(tile * rows, 8), rows)], own_sem)
    own.start()

    def on_z(step, way, part):
        item = (step, way)

        def body():
            z_arrival(step, way, part).wait_recv()
            if step + 1 < nz:
                when(z_sends(step + 1, way), lambda: z_copy(step + 1, way, part).start())
            y_copy(0, item, part).start()
            if part == MINE:
                x_copy(0, item).start()
            c_copy(0, item, part).start()

        when(there(item), body)

    def on_y(item, part):
        def body():
            y_copy(1, item, part).wait_recv()
            if part == MINE:
                x_copy(1, item).start()
            c_copy(1, item, part).start()

        when(there(item), body)

    def on_x(column, item):
        def body():
            x_copy(column, item, OTHER).wait_recv()
            c_copy(column, item, OTHER).start()

        when(there(item), body)

    def at_step(step):
        return [item for item in items if item[0] == step]

    block = rows_in.shape[0]

    def solve_rows(at):
        here = pl.ds(at * block, block)
        fetch = pltpu.make_async_copy(panel.at[here], rows_in, in_sem)
        fetch.start()
        fetch.wait()
        rows_out[...] = matmul(rows_in[...], inverse[...], True)
        store = pltpu.make_async_copy(rows_out, factors.at[here], out_sem)
        store.start()
        store.wait()

    stages = pivot_stages(pivot_blocks, coupling, inverse, diagonal, work, lower, schur, solve, coupled)
    stages += [(2.2, functools.partial(solve_rows, at)) for at in range(rows // block)]
    total = sum(weight for weight, _ in stages)
    done, gap = 0.0, 0

    def arithmetic():
        nonlocal done, gap
        gap += 1
        while stages and (done < total * gap / (2 * nz) or gap == 2 * nz):
            weight, stage = stages.pop(0)
            stage()
            done += weight

    for step in range(1, nz + 1):
        for part in (MINE, SHARED):
            arithmetic()
            if step < nz:
                for way in (0, 1):
                    on_z(step, way, part)
            for item in at_step(step - 1):
                on_y(item, part)
        if step < nz:
            for item in at_step(step - 1):
                if step > 1:
                    on_x(0, item)
            for item in at_step(step - 2):
                on_x(1, item)
    for item in at_step(nz - 1):
        on_x(0, item)
    for step in (nz - 2, nz - 1):
        for item in at_step(step):
            on_x(1, item)

    for column in (0, 1):
        for item in items:
            if column == 0 and item == (0, 0):
                continue

            def finish():
                for part in (MINE, SHARED, OTHER):
                    c_arrival(column, item, part).wait_recv()
                    c_copy(column, item, part).wait_send()
                x_copy(column, item).wait_send()

            when(there(item), finish)
    for item in items:
        for part in (MINE, SHARED):
            when(there(item), lambda: y_copy(0, item, part).wait_send())
            for way in (0, 1):
                if item[0] + 1 < nz and (item[0] == 0 or item[1] == way):
                    step = item[0] + 1
                    when(z_sends(step, way), lambda: z_copy(step, way, part).wait_send())
    own.wait()


def spread(panel, pivot_blocks, coupling, mesh):
    n_tiles, n_rep = mesh.shape["tiles"], mesh.shape["rep"]
    assert n_tiles % 2 == 0 and n_rep == 4
    nz = n_tiles // 2
    rows, width = panel.shape
    half = rows // 2
    alone = half // 48 * 17 // 8 * 8
    sizes = (nz, rows, half, alone, half - 2 * alone)
    n_items = 2 * nz - 1
    dma = lambda n: pltpu.SemaphoreType.DMA((n,))
    block = coupling.shape[0]
    any_space, vmem = pl.BlockSpec(memory_space=pl.ANY), pl.BlockSpec(memory_space=pltpu.VMEM)
    f32 = lambda *shape: jax.ShapeDtypeStruct(shape, jnp.float32)
    buffer = lambda *shape: pltpu.VMEM(shape, jnp.float32)
    return pl.pallas_call(
        functools.partial(spread_kernel, sizes),
        out_shape=(f32(n_tiles * rows, width), f32(width, width), f32(*pivot_blocks.shape[:2]), f32(rows, width)),
        in_specs=[any_space, vmem, vmem],
        out_specs=(any_space, vmem, vmem, any_space),
        scratch_shapes=[dma(4 * max(nz - 1, 1))] * 2 + [dma(2 * n_items)] * 2 + [dma(2 * n_items)] * 2
        + [dma(6 * n_items)] * 2 + [pltpu.SemaphoreType.DMA]
        + [buffer(block // 2, block), buffer(block // 2, block // 2)] + [buffer(block, block)] * 3
        + [buffer(block, width)] * 2 + [pltpu.SemaphoreType.DMA] * 2,
        compiler_params=pltpu.CompilerParams(
            collective_id=0, has_side_effects=True, vmem_limit_bytes=40 << 20),
        name="spread_rows",
    )(panel, pivot_blocks, coupling)


def halves(value):
    high = value.astype(jnp.bfloat16)
    low = (value - high.astype(jnp.float32)).astype(jnp.bfloat16)
    return high, low


def split_product(stacked, right, dims):
    rows = stacked.shape[0] // 2
    high, low = halves(right)
    dot = functools.partial(lax.dot_general, dimension_numbers=(dims, ((), ())), preferred_element_type=jnp.float32)
    first = dot(stacked, high)
    return first[:rows] + (first[rows:] + dot(stacked[:rows], low))


def update_kernel(per_step, pairs, source, tiles, gram, every_row, *refs):
    rows, (out, weights, raw, sems) = refs[:per_step], refs[per_step:]
    step = pl.program_id(0)

    @pl.when(step == 0)
    def _():
        def fetch(at):
            return pltpu.make_async_copy(every_row.at[jnp.maximum(source[at], 0)], raw.at[at], sems.at[at])

        for at in range(LEFT):
            fetch(at).start()
        weights[LEFT] = jnp.zeros(weights.shape[1:], weights.dtype)

        def make(at, carry):
            fetch(at).wait()
            stacked = jnp.concatenate(halves(raw[at]), axis=0)
            product = split_product(stacked, gram[...], ((1,), (0,)))
            weights[at] = jnp.concatenate(halves(product), axis=0)
            return carry

        lax.fori_loop(0, LEFT, make, 0)

    for at in range(per_step):
        slot = step * per_step + at
        left, right = pairs[2 * slot], pairs[2 * slot + 1]
        used = jnp.logical_and(source[left] >= 0, source[right] >= 0)
        chosen = jnp.where(used, jnp.minimum(left, LEFT), LEFT)
        out[at] = tiles[at] - split_product(weights[chosen], rows[at][0], ((1,), (1,)))


def update(tiles, gram, every_row, pairs, source):
    slots, block, _ = tiles.shape
    width = every_row.shape[2]
    per_step = next(n for n in (5, 4, 3, 2, 1) if slots % n == 0)

    def row_spec(at):
        def place(i, pairs, source):
            return jnp.maximum(source[pairs[2 * (i * per_step + at) + 1]], 0), 0, 0

        return pl.BlockSpec((1, block, width), place)

    tile_spec = pl.BlockSpec((per_step, block, block), lambda i, p, s: (i, 0, 0))
    return pl.pallas_call(
        functools.partial(update_kernel, per_step),
        grid_spec=pltpu.PrefetchScalarGridSpec(
            num_scalar_prefetch=2, grid=(slots // per_step,),
            in_specs=[tile_spec, pl.BlockSpec((width, width), lambda i, p, s: (0, 0)),
                      pl.BlockSpec(memory_space=pl.ANY)] + [row_spec(at) for at in range(per_step)],
            out_specs=tile_spec,
            scratch_shapes=[pltpu.VMEM((LEFT + 1, 2 * block, width), jnp.bfloat16),
                            pltpu.VMEM((LEFT, block, width), jnp.float32),
                            pltpu.SemaphoreType.DMA((LEFT,))],
        ),
        out_shape=jax.ShapeDtypeStruct(tiles.shape, tiles.dtype),
        compiler_params=pltpu.CompilerParams(vmem_limit_bytes=48 << 20),
        name="update_tiles",
    )(pairs, source, tiles, gram, every_row, *[every_row] * per_step)


def per_device(mesh, trailing_tiles, panel_rows, pivot_blocks, coupling, row_ids, membership, tile_pairs):
    owned, block, width = panel_rows.shape
    tile_index = lax.axis_index("tiles")
    own_ids = lax.dynamic_slice_in_dim(row_ids, tile_index * owned, owned)
    wanted = lax.dynamic_index_in_dim(membership, tile_index, 0, keepdims=False)
    found = jnp.argmax(row_ids[None, :] == wanted[:, None], axis=1).astype(jnp.int32)
    source = jnp.pad(jnp.where(wanted < NB, found, -1), (0, 1), constant_values=-1)
    every_row, inverse, diagonal, factors = spread(
        panel_rows.reshape(owned * block, width), pivot_blocks, coupling, mesh)
    every_row = every_row.reshape(-1, block, width)
    factors = factors.reshape(panel_rows.shape)
    factors = jnp.where((own_ids < NB)[:, None, None], factors, jnp.zeros_like(factors))
    gram = jnp.dot((inverse * diagonal.reshape(-1, 1)).T, inverse, precision=HI)
    updated = update(trailing_tiles, gram, every_row, tile_pairs.reshape(-1), source)
    return (updated, factors, diagonal)


def solution(mesh):
    return jax.shard_map(
        functools.partial(per_device, mesh),
        mesh=mesh,
        in_specs=(
            P(("tiles", "rep"), None, None),
            P("tiles", None, None),
            P(),
            P(),
            P(),
            P(),
            P(("tiles", "rep"), None),
        ),
        out_specs=(P(("tiles", "rep"), None, None), P("tiles", None, None), P()),
        check_vma=False,
    )
```
